32 devices in a mesh: dp: 2 (over y), expert: 16 (over z, x, core).
Axes of the slice: x: 2, y: 2, z: 4, core: 2. Of those that a mesh axis runs over, the one named last changes fastest.
Arguments:
- tokens: bfloat16 [512, 4096], P('expert', 'dp'), may hold values from -6 to 6
- expert_ids: int32 [512, 8], P('expert'), may hold values from 0 to 15, all different within a row; in each aligned block of 32 rows (0 to 31, 32 to 63, ...) at most 32 rows name the same one
- route_weights: float32 [512, 8], P('expert'), may hold values from 0.05 to 0.3
- cotangent: bfloat16 [512, 4096], P('expert', 'dp'), may hold values from -6 to 6
- w_gate: bfloat16 [16, 4096, 1536], P('expert', 'dp'), may hold values from -0.09375 to 0.09375
- w_up: bfloat16 [16, 4096, 1536], P('expert', 'dp'), may hold values from -0.09375 to 0.09375
- w_down: bfloat16 [16, 1536, 4096], P('expert', None, 'dp'), may hold values from -0.15625 to 0.15625
Outputs:
- mixed: bfloat16 [512, 4096], P('expert', 'dp')
- token_grad: bfloat16 [512, 4096], P('expert', 'dp')
- down_grad: bfloat16 [16, 1536, 4096], P('expert', None, 'dp')
The draws below stay inside these ranges and needn't reach their ends.
Inputs may be any that keep to these rules, and one draw needn't show every extreme that they name: `expert_ids`: each row names 8 different experts. Among the 32 rows of one token group no expert is named more than 32 times, a bound that some block reaches.
All inputs are finite; a program needn't handle non-finite values.
Results may differ from the reference program's by a relative error of at most 0.015.
Values may be sent and summed in bfloat16 or wider, within the bound.
A program may use at most 128 MiB of HBM per device.

```python
import math
import jax
import jax.numpy as jnp
import numpy as np
from jax import lax

D = 4096
FF = 1536
TOPK = 8
TOK_DEV = 32
EXPERTS = 16
CAP = 32
TOKENS = 512
N_DP = 2


def shard_levels(rng, extent, cuts, smallest, largest):
    gain, own = 1.0, jax.random.fold_in(rng, 6)
    for axis_at, parts in cuts:
        steps = jnp.exp(jax.random.uniform(jax.random.fold_in(own, axis_at), (parts,), jnp.float32, smallest / len(cuts), largest / len(cuts)))
        gain = gain * jnp.repeat(steps, extent[axis_at] // parts).reshape([-1 if axis == axis_at else 1 for axis in range(len(extent))])
    return gain


def shared_out(own_key, own, number, rows, count, top, most, skew):
    ranking = jax.random.permutation(own_key, count)
    heavy_load, ordinary = shares(count, rows * top, most, skew, True), shares(count, rows * top, most, skew, False)
    places = jnp.arange(count)

    def named(tallies, rotation):
        used = int((tallies > 0).sum())
        fixed = max(1, used // 4)
        moved = fixed + (places - fixed + rotation * (used - fixed)) % max(1, count - fixed)
        return jnp.zeros((count,), jnp.int32).at[ranking[jnp.where(places < fixed, places, moved)]].set(jnp.asarray(tallies, jnp.int32))

    tallies = jnp.where(number % 4 == 0, named(heavy_load, number // 4), named(ordinary, number - number // 4 - 1))
    mixed = jax.random.permutation(jax.random.fold_in(own, 3), count)
    giver, taker = mixed[0:count // 2 * 2:2], mixed[1:count // 2 * 2:2]
    room = jnp.minimum(tallies[giver] - 1, most - tallies[taker]) // 2
    room = jnp.where((giver == ranking[0]) | (taker == ranking[0]) | (tallies[taker] == 0), 0, jnp.maximum(room, 0))
    moved = jax.random.randint(jax.random.fold_in(own, 4), (count // 2,), 0, 1 << 20) % (room + 1)
    tallies = tallies.at[giver].add(-moved).at[taker].add(moved)
    members = jnp.searchsorted(jnp.cumsum(tallies), jnp.arange(rows * top), side="right").astype(jnp.int32)
    table = members.reshape(top, rows).T
    table = table[jax.random.permutation(jax.random.fold_in(own, 1), rows)]
    rotation = jax.random.randint(jax.random.fold_in(own, 2), (rows, 1), 0, top)
    return jnp.take_along_axis(table, (jnp.arange(top)[None, :] + rotation) % top, axis=1)


def shares(count, total, reach, skew, full):
    weights = [(1 << 20) // math.isqrt(standing ** skew) + 1 for standing in range(1, count + 1)]
    largest = reach if full else min(reach, max(-(-total // count), total * weights[0] // sum(weights)))
    least = 1 if total - largest >= count - 1 else 0
    counts, spare = [largest] + [least] * (count - 1), total - largest - least * (count - 1)
    while spare > 0:
        candidates = [i for i in range(1, count) if counts[i] < largest] or [i for i in range(1, count) if counts[i] < reach]
        mass, left = sum([weights[i] for i in candidates]), spare
        for i in candidates:
            extra = min(reach - counts[i], max(1, left * weights[i] // mass), spare)
            counts[i] = counts[i] + extra
            spare = spare - extra
    return np.array(counts)


def noise(rng, shape, scale, most, split=(), kind=jnp.bfloat16):
    values = jax.random.normal(rng, shape, jnp.float32) * scale
    if len(split) > 0:
        values = shard_levels(rng, shape, split, -0.22, 0.18) * values
    return jnp.clip(values, min=-most, max=most).astype(kind)


def setup_inputs(seed: int = 0) -> dict:
    arg_keys = jax.random.split(jax.random.key(seed), 8)
    tokens = noise(arg_keys[0], (TOKENS, D), 1.0, 6.0, ((0, 16), (1, 2)))
    expert_ids_keys = jax.random.split(jax.random.fold_in(arg_keys[1], 1), TOKENS // TOK_DEV)
    expert_ids_turns = jax.random.permutation(jax.random.fold_in(arg_keys[1], 3), TOKENS // TOK_DEV)
    expert_ids = jax.vmap(lambda own, number: shared_out(jax.random.fold_in(arg_keys[1], 2), own, number, TOK_DEV, EXPERTS, TOPK, CAP, 2))(expert_ids_keys, expert_ids_turns).reshape((TOKENS, TOPK))
    route_weights = jnp.clip(0.05 + 0.25 * jax.random.uniform(arg_keys[2], (TOKENS, TOPK), jnp.float32) ** shard_levels(arg_keys[2], (TOKENS, TOPK), ((0, 16),), -0.2, 0.2), 0.05, 0.3)
    cotangent = noise(arg_keys[3], (TOKENS, D), 1.0, 6.0, ((0, 16), (1, 2)))
    w_gate = noise(arg_keys[4], (EXPERTS, D, FF), D ** -0.5, 0.09375, ((0, 16), (1, 2)))
    w_up = noise(arg_keys[5], (EXPERTS, D, FF), D ** -0.5, 0.09375, ((0, 16), (1, 2)))
    w_down = noise(arg_keys[6], (EXPERTS, FF, D), FF ** -0.5, 0.15625, ((0, 16), (2, 2)))
    return {"tokens": tokens, "expert_ids": expert_ids, "route_weights": route_weights, "cotangent": cotangent, "w_gate": w_gate, "w_up": w_up, "w_down": w_down}


def pointwise(gate_pre, up_pre, grad_hidden):
    sigmoid_g = jax.nn.sigmoid(gate_pre)
    activation = gate_pre * sigmoid_g
    hidden = (activation * up_pre).astype(jnp.bfloat16)
    slope = sigmoid_g * (1.0 + gate_pre * (1.0 - sigmoid_g))
    grad_gate = (grad_hidden * up_pre * slope).astype(jnp.bfloat16)
    grad_up = (grad_hidden * activation).astype(jnp.bfloat16)
    return hidden, grad_gate, grad_up


def piece_sum(products):
    rounded = products.astype(jnp.bfloat16)
    rounded = lax.optimization_barrier(rounded)
    return jnp.sum(rounded.astype(jnp.float32), axis=1)


def one_expert(inputs):
    routed_x, routed_dy, gate_w, up_w, down_w = inputs
    row_total = routed_x.shape[0] * routed_x.shape[1]
    piece_width = D // N_DP
    rows_x = routed_x.reshape(row_total, N_DP, piece_width).astype(jnp.float32)
    rows_dy = routed_dy.reshape(row_total, N_DP, piece_width).astype(jnp.float32)
    gate_p = gate_w.reshape(N_DP, piece_width, FF).astype(jnp.float32)
    up_p = up_w.reshape(N_DP, piece_width, FF).astype(jnp.float32)
    down_p = down_w.reshape(FF, N_DP, piece_width).astype(jnp.float32)
    gate_pre = piece_sum(jnp.einsum("rjd,jdf->rjf", rows_x, gate_p))
    up_pre = piece_sum(jnp.einsum("rjd,jdf->rjf", rows_x, up_p))
    grad_hidden = piece_sum(jnp.einsum("rjd,fjd->rjf", rows_dy, down_p))
    hidden, grad_gate, grad_up = pointwise(gate_pre, up_pre, grad_hidden)
    expert_out = jnp.dot(hidden, down_w, preferred_element_type=jnp.float32).astype(jnp.bfloat16)
    grad_rows = lax.dot_general(grad_gate, gate_w, (((1,), (1,)), ((), ())), preferred_element_type=jnp.float32)
    grad_rows = grad_rows + lax.dot_general(grad_up, up_w, (((1,), (1,)), ((), ())), preferred_element_type=jnp.float32)
    flat_dy = routed_dy.reshape(row_total, D)
    down_g = lax.dot_general(hidden, flat_dy, (((0,), (0,)), ((), ())), preferred_element_type=jnp.float32)
    shape_back = routed_x.shape
    return expert_out.reshape(shape_back), grad_rows.astype(jnp.bfloat16).reshape(shape_back), down_g.astype(jnp.bfloat16)


def reference(tokens, expert_ids, route_weights, cotangent, w_gate, w_up, w_down):
    groups = TOKENS // TOK_DEV
    pair_count = TOK_DEV * TOPK
    group_ids = expert_ids.reshape(groups, pair_count)
    onehot = (group_ids[:, :, None] == jnp.arange(EXPERTS, dtype=jnp.int32)[None, None, :]).astype(jnp.int32)
    position = jnp.sum((jnp.cumsum(onehot, axis=1) - onehot) * onehot, axis=2).astype(jnp.int32)
    group_index = jnp.arange(groups, dtype=jnp.int32)[:, None]
    token_index = (jnp.arange(pair_count, dtype=jnp.int32)[None, :] // TOPK + group_index * TOK_DEV).astype(jnp.int32)
    source_index = jnp.broadcast_to(group_index, (groups, pair_count)).astype(jnp.int32)
    pair_weights = route_weights.reshape(groups, pair_count)
    x_pairs = tokens[token_index]
    dy_pairs = (cotangent[token_index].astype(jnp.float32) * pair_weights[:, :, None]).astype(jnp.bfloat16)
    routed_x = jnp.zeros((EXPERTS, groups, CAP, D), jnp.bfloat16).at[group_ids, source_index, position].set(x_pairs)
    routed_dy = jnp.zeros((EXPERTS, groups, CAP, D), jnp.bfloat16).at[group_ids, source_index, position].set(dy_pairs)
    expert_out, grad_rows, down_grad = lax.map(one_expert, (routed_x, routed_dy, w_gate, w_up, w_down))
    out_pairs = expert_out[group_ids, source_index, position].astype(jnp.float32)
    grad_pairs = grad_rows[group_ids, source_index, position].astype(jnp.float32)
    mixed = jnp.sum((out_pairs * pair_weights[:, :, None]).reshape(groups, TOK_DEV, TOPK, D), axis=2)
    token_grad = jnp.sum(grad_pairs.reshape(groups, TOK_DEV, TOPK, D), axis=2)
    return mixed.reshape(TOKENS, D).astype(jnp.bfloat16), token_grad.reshape(TOKENS, D).astype(jnp.bfloat16), down_grad
```

```python
import jax
import jax.numpy as jnp
from jax import lax
from jax.sharding import PartitionSpec as P


def pointwise(gate_pre, up_pre, grad_hidden):
    sigmoid_g = jax.nn.sigmoid(gate_pre)
    activation = gate_pre * sigmoid_g
    hidden = (activation * up_pre).astype(jnp.bfloat16)
    slope = sigmoid_g * (1.0 + gate_pre * (1.0 - sigmoid_g))
    grad_gate = (grad_hidden * up_pre * slope).astype(jnp.bfloat16)
    grad_up = (grad_hidden * activation).astype(jnp.bfloat16)
    return (hidden, grad_gate, grad_up)


def split_sums(full_sums, hidden_width):
    return pointwise(
        full_sums[:, :hidden_width],
        full_sums[:, hidden_width : 2 * hidden_width],
        full_sums[:, 2 * hidden_width :],
    )


def shards_slots(tokens, expert_ids, route_weights, cotangent, w_gate, w_up, w_down):
    tok_rows, feat_width = tokens.shape
    top_count = expert_ids.shape[1]
    expert_count = lax.axis_size("expert")
    capacity = min(tok_rows, 2 * tok_rows * top_count // expert_count)
    slots_total = expert_count * capacity
    pair_count = tok_rows * top_count
    flat_ids = expert_ids.reshape(pair_count)
    onehot = (flat_ids[:, None] == jnp.arange(expert_count, dtype=jnp.int32)[None, :]).astype(
        jnp.int32
    )
    position = jnp.sum((jnp.cumsum(onehot, axis=0) - onehot) * onehot, axis=1)
    slot_index = flat_ids * capacity + position
    chosen = slot_index[:, None] == jnp.arange(slots_total, dtype=jnp.int32)[None, :]
    chosen_b = chosen.astype(jnp.bfloat16)
    x_pairs = jnp.repeat(tokens, top_count, axis=0)
    pair_weights = route_weights.reshape(pair_count, 1)
    dy_pairs = (jnp.repeat(cotangent, top_count, axis=0).astype(jnp.float32) * pair_weights).astype(
        jnp.bfloat16
    )
    contract_pairs = (((0,), (0,)), ((), ()))
    send_x = lax.dot_general(
        chosen_b, x_pairs, contract_pairs, preferred_element_type=jnp.float32
    ).astype(jnp.bfloat16)
    send_dy = lax.dot_general(
        chosen_b, dy_pairs, contract_pairs, preferred_element_type=jnp.float32
    ).astype(jnp.bfloat16)
    recv_x, recv_dy = (
        lax.all_to_all(
            send_x.reshape(expert_count, capacity, feat_width),
            "expert",
            split_axis=0,
            concat_axis=0,
            tiled=True,
        ),
        lax.all_to_all(
            send_dy.reshape(expert_count, capacity, feat_width),
            "expert",
            split_axis=0,
            concat_axis=0,
            tiled=True,
        ),
    )
    rows_x = recv_x.reshape(slots_total, feat_width)
    rows_dy = recv_dy.reshape(slots_total, feat_width)
    gate_local = w_gate[0]
    up_local = w_up[0]
    down_local = w_down[0]
    hidden_width = gate_local.shape[1]
    contract_last = (((1,), (1,)), ((), ()))
    gate_part = jnp.dot(rows_x, gate_local, preferred_element_type=jnp.float32)
    up_part = jnp.dot(rows_x, up_local, preferred_element_type=jnp.float32)
    back_part = lax.dot_general(
        rows_dy, down_local, contract_last, preferred_element_type=jnp.float32
    )
    row_share = lax.psum_scatter(
        jnp.concatenate([gate_part, up_part, back_part], axis=1).astype(jnp.bfloat16),
        "dp",
        scatter_dimension=0,
        tiled=True,
    ).astype(jnp.float32)
    hidden_s, gate_s, up_s = split_sums(row_share, hidden_width)
    hidden, grad_gate, grad_up = (
        lax.all_gather(hidden_s, "dp", axis=0, tiled=True),
        lax.all_gather(gate_s, "dp", axis=0, tiled=True),
        lax.all_gather(up_s, "dp", axis=0, tiled=True),
    )
    expert_out = jnp.dot(hidden, down_local, preferred_element_type=jnp.float32).astype(
        jnp.bfloat16
    )
    grad_rows = lax.dot_general(
        grad_gate, gate_local, contract_last, preferred_element_type=jnp.float32
    )
    grad_rows = (
        grad_rows
        + lax.dot_general(grad_up, up_local, contract_last, preferred_element_type=jnp.float32)
    ).astype(jnp.bfloat16)
    down_grad = lax.dot_general(
        hidden, rows_dy, contract_pairs, preferred_element_type=jnp.float32
    ).astype(jnp.bfloat16)
    back_out, back_grad = (
        lax.all_to_all(
            expert_out.reshape(expert_count, capacity, feat_width),
            "expert",
            split_axis=0,
            concat_axis=0,
            tiled=True,
        ),
        lax.all_to_all(
            grad_rows.reshape(expert_count, capacity, feat_width),
            "expert",
            split_axis=0,
            concat_axis=0,
            tiled=True,
        ),
    )
    weighted_sel = (
        (chosen.astype(jnp.float32) * pair_weights)
        .reshape(tok_rows, top_count, slots_total)
        .sum(axis=1)
    )
    plain_sel = chosen_b.reshape(tok_rows, top_count, slots_total).sum(axis=1)
    mixed = jnp.dot(
        weighted_sel,
        back_out.reshape(slots_total, feat_width).astype(jnp.float32),
        precision=lax.Precision.HIGHEST,
    ).astype(jnp.bfloat16)
    token_grad = jnp.dot(
        plain_sel, back_grad.reshape(slots_total, feat_width), preferred_element_type=jnp.float32
    ).astype(jnp.bfloat16)
    return (mixed, token_grad, down_grad[None])


CHUNKS = 2


def gather_rows(block):
    return lax.all_gather(block, "expert", axis=0, tiled=True)


def scatter_sum(rows):
    parts = lax.all_to_all(
        rows.reshape(lax.axis_size("expert"), -1, rows.shape[1]), "expert", 0, 0, tiled=True
    )
    return jnp.sum(parts.astype(jnp.float32), axis=0).astype(jnp.bfloat16)


def swap_pieces(block):
    return lax.ppermute(block, "dp", [(0, 1), (1, 0)])


def shards_dense(tokens, expert_ids, route_weights, cotangent, w_gate, w_up, w_down):
    tok_rows, feat_width = tokens.shape
    expert_count = lax.axis_size("expert")
    chunks = CHUNKS
    step = tok_rows // chunks
    me = lax.axis_index("expert")
    named = expert_ids[:, :, None] == jnp.arange(expert_count, dtype=jnp.int32)[None, None, :]
    dense = jnp.sum(jnp.where(named, route_weights[:, :, None], 0.0), axis=1)
    all_weights = gather_rows(dense)
    mine = lax.dynamic_slice_in_dim(all_weights, me, 1, axis=1).reshape(
        expert_count, chunks, step
    )
    gate_local, up_local, down_local = w_gate[0], w_up[0], w_down[0]
    last = (((1,), (1,)), ((), ()))
    first = (((0,), (0,)), ((), ()))
    f32 = jnp.float32
    xs = [gather_rows(tokens[c * step : (c + 1) * step]) for c in range(chunks)]
    cs = [gather_rows(cotangent[c * step : (c + 1) * step]) for c in range(chunks)]
    ws = [mine[:, c, :].reshape(expert_count * step, 1) for c in range(chunks)]
    hiddens, dys, mixed, token_grad = [], [], [], []
    for c in range(chunks):
        rows_x = xs[c]
        gate_part = jnp.dot(rows_x, gate_local, preferred_element_type=f32).astype(jnp.bfloat16)
        gate_other = swap_pieces(gate_part)
        up_part = jnp.dot(rows_x, up_local, preferred_element_type=f32).astype(jnp.bfloat16)
        up_other = swap_pieces(up_part)
        rows_dy = (cs[c].astype(f32) * ws[c]).astype(jnp.bfloat16)
        back_part = lax.dot_general(rows_dy, down_local, last, preferred_element_type=f32).astype(
            jnp.bfloat16
        )
        back_other = swap_pieces(back_part)
        hidden, grad_gate, grad_up = pointwise(
            gate_part.astype(f32) + gate_other.astype(f32),
            up_part.astype(f32) + up_other.astype(f32),
            back_part.astype(f32) + back_other.astype(f32),
        )
        out = jnp.dot(hidden, down_local, preferred_element_type=f32)
        mixed.append(scatter_sum((out * ws[c]).astype(jnp.bfloat16)))
        grad = lax.dot_general(grad_gate, gate_local, last, preferred_element_type=f32)
        grad = grad + lax.dot_general(grad_up, up_local, last, preferred_element_type=f32)
        token_grad.append(scatter_sum(grad.astype(jnp.bfloat16)))
        hiddens.append(hidden)
        dys.append(rows_dy)
    down_grad = lax.dot_general(
        jnp.concatenate(hiddens, axis=0),
        jnp.concatenate(dys, axis=0),
        first,
        preferred_element_type=f32,
    ).astype(jnp.bfloat16)
    return (
        jnp.concatenate(mixed, axis=0),
        jnp.concatenate(token_grad, axis=0),
        down_grad[None],
    )


def shards(tokens, expert_ids, *rest):
    tok_rows, top_count = expert_ids.shape
    expert_count = lax.axis_size("expert")
    capacity = min(tok_rows, 2 * tok_rows * top_count // expert_count)
    body = shards_dense if capacity == tok_rows else shards_slots
    return body(tokens, expert_ids, *rest)


def solution(mesh):
    return jax.shard_map(
        shards,
        mesh=mesh,
        in_specs=(
            P("expert", "dp"),
            P("expert", None),
            P("expert", None),
            P("expert", "dp"),
            P("expert", "dp", None),
            P("expert", "dp", None),
            P("expert", None, "dp"),
        ),
        out_specs=(P("expert", "dp"), P("expert", "dp"), P("expert", None, "dp")),
        check_vma=False,
    )
```

```python
import functools

import jax
import jax.numpy as jnp
from jax import lax
from jax.experimental import pallas as pl
from jax.experimental.pallas import tpu as pltpu
from jax.sharding import PartitionSpec as P


def pointwise(gate_pre, up_pre, grad_hidden):
    sigmoid_g = jax.nn.sigmoid(gate_pre)
    activation = gate_pre * sigmoid_g
    hidden = (activation * up_pre).astype(jnp.bfloat16)
    slope = sigmoid_g * (1.0 + gate_pre * (1.0 - sigmoid_g))
    grad_gate = (grad_hidden * up_pre * slope).astype(jnp.bfloat16)
    grad_up = (grad_hidden * activation).astype(jnp.bfloat16)
    return (hidden, grad_gate, grad_up)


def split_sums(full_sums, hidden_width):
    return pointwise(
        full_sums[:, :hidden_width],
        full_sums[:, hidden_width : 2 * hidden_width],
        full_sums[:, 2 * hidden_width :],
    )


def shards_slots(tokens, expert_ids, route_weights, cotangent, w_gate, w_up, w_down):
    tok_rows, feat_width = tokens.shape
    top_count = expert_ids.shape[1]
    expert_count = lax.axis_size("expert")
    capacity = min(tok_rows, 2 * tok_rows * top_count // expert_count)
    slots_total = expert_count * capacity
    pair_count = tok_rows * top_count
    flat_ids = expert_ids.reshape(pair_count)
    onehot = (flat_ids[:, None] == jnp.arange(expert_count, dtype=jnp.int32)[None, :]).astype(
        jnp.int32
    )
    position = jnp.sum((jnp.cumsum(onehot, axis=0) - onehot) * onehot, axis=1)
    slot_index = flat_ids * capacity + position
    chosen = slot_index[:, None] == jnp.arange(slots_total, dtype=jnp.int32)[None, :]
    chosen_b = chosen.astype(jnp.bfloat16)
    x_pairs = jnp.repeat(tokens, top_count, axis=0)
    pair_weights = route_weights.reshape(pair_count, 1)
    dy_pairs = (jnp.repeat(cotangent, top_count, axis=0).astype(jnp.float32) * pair_weights).astype(
        jnp.bfloat16
    )
    contract_pairs = (((0,), (0,)), ((), ()))
    send_x = lax.dot_general(
        chosen_b, x_pairs, contract_pairs, preferred_element_type=jnp.float32
    ).astype(jnp.bfloat16)
    send_dy = lax.dot_general(
        chosen_b, dy_pairs, contract_pairs, preferred_element_type=jnp.float32
    ).astype(jnp.bfloat16)
    recv_x, recv_dy = (
        lax.all_to_all(
            send_x.reshape(expert_count, capacity, feat_width),
            "expert",
            split_axis=0,
            concat_axis=0,
            tiled=True,
        ),
        lax.all_to_all(
            send_dy.reshape(expert_count, capacity, feat_width),
            "expert",
            split_axis=0,
            concat_axis=0,
            tiled=True,
        ),
    )
    rows_x = recv_x.reshape(slots_total, feat_width)
    rows_dy = recv_dy.reshape(slots_total, feat_width)
    gate_local = w_gate[0]
    up_local = w_up[0]
    down_local = w_down[0]
    hidden_width = gate_local.shape[1]
    contract_last = (((1,), (1,)), ((), ()))
    gate_part = jnp.dot(rows_x, gate_local, preferred_element_type=jnp.float32)
    up_part = jnp.dot(rows_x, up_local, preferred_element_type=jnp.float32)
    back_part = lax.dot_general(
        rows_dy, down_local, contract_last, preferred_element_type=jnp.float32
    )
    row_share = lax.psum_scatter(
        jnp.concatenate([gate_part, up_part, back_part], axis=1).astype(jnp.bfloat16),
        "dp",
        scatter_dimension=0,
        tiled=True,
    ).astype(jnp.float32)
    hidden_s, gate_s, up_s = split_sums(row_share, hidden_width)
    hidden, grad_gate, grad_up = (
        lax.all_gather(hidden_s, "dp", axis=0, tiled=True),
        lax.all_gather(gate_s, "dp", axis=0, tiled=True),
        lax.all_gather(up_s, "dp", axis=0, tiled=True),
    )
    expert_out = jnp.dot(hidden, down_local, preferred_element_type=jnp.float32).astype(
        jnp.bfloat16
    )
    grad_rows = lax.dot_general(
        grad_gate, gate_local, contract_last, preferred_element_type=jnp.float32
    )
    grad_rows = (
        grad_rows
        + lax.dot_general(grad_up, up_local, contract_last, preferred_element_type=jnp.float32)
    ).astype(jnp.bfloat16)
    down_grad = lax.dot_general(
        hidden, rows_dy, contract_pairs, preferred_element_type=jnp.float32
    ).astype(jnp.bfloat16)
    back_out, back_grad = (
        lax.all_to_all(
            expert_out.reshape(expert_count, capacity, feat_width),
            "expert",
            split_axis=0,
            concat_axis=0,
            tiled=True,
        ),
        lax.all_to_all(
            grad_rows.reshape(expert_count, capacity, feat_width),
            "expert",
            split_axis=0,
            concat_axis=0,
            tiled=True,
        ),
    )
    weighted_sel = (
        (chosen.astype(jnp.float32) * pair_weights)
        .reshape(tok_rows, top_count, slots_total)
        .sum(axis=1)
    )
    plain_sel = chosen_b.reshape(tok_rows, top_count, slots_total).sum(axis=1)
    mixed = jnp.dot(
        weighted_sel,
        back_out.reshape(slots_total, feat_width).astype(jnp.float32),
        precision=lax.Precision.HIGHEST,
    ).astype(jnp.bfloat16)
    token_grad = jnp.dot(
        plain_sel, back_grad.reshape(slots_total, feat_width), preferred_element_type=jnp.float32
    ).astype(jnp.bfloat16)
    return (mixed, token_grad, down_grad[None])


CHUNKS = 2


def gather_kernel(depth, count, *refs):
    ins, outs = refs[:count], refs[count : 2 * count]
    send_sem, recv_sem, own_sem = refs[2 * count :]
    me, piece = lax.axis_index("expert"), lax.axis_index("dp")
    z, x, core = me // 4, (me // 2) % 2, me % 2

    def place(z_at, x_at, core_at):
        return (z_at * 2 + x_at) * 2 + core_at

    across, sibling = place(z, 1 - x, core), place(z, x, 1 - core)
    along = [place(lax.rem(z + k, depth), x, core) for k in range(1, depth)]
    barrier = pltpu.get_barrier_semaphore()
    for peer in [*along, across, sibling]:
        pl.semaphore_signal(
            barrier, inc=1, device_id=(piece, peer), device_id_type=pl.DeviceIdType.MESH
        )
    pl.semaphore_wait(barrier, depth + 1)

    def copy(a, src, slot, sem, peer):
        return pltpu.make_async_remote_copy(
            src_ref=src,
            dst_ref=outs[a].at[slot],
            send_sem=send_sem.at[a, sem],
            recv_sem=recv_sem.at[a, sem],
            device_id=(piece, peer),
            device_id_type=pl.DeviceIdType.MESH,
        )

    own, started = [], []
    x_step = {}
    core_step = {}
    z_step = {}
    for a in range(count):
        own.append(pltpu.make_async_copy(ins[a], outs[a].at[me], own_sem.at[a]))
        own[-1].start()
        for k in range(1, depth):
            z_step[a, k] = copy(a, ins[a], me, k - 1, along[k - 1])
            z_step[a, k].start()
        x_step[a, 0] = copy(a, ins[a], me, depth - 1, across)
        x_step[a, 0].start()
        core_step[a, 0] = copy(a, ins[a], me, 2 * depth - 1, sibling)
        core_step[a, 0].start()
    for k in range(1, depth):
        for a in range(count):
            z_step[a, k].wait_recv()
            slot = place(lax.rem(z + depth - k, depth), x, core)
            x_step[a, k] = copy(a, outs[a].at[slot], slot, depth - 1 + k, across)
            x_step[a, k].start()
            core_step[a, k] = copy(a, outs[a].at[slot], slot, 2 * depth - 1 + k, sibling)
            core_step[a, k].start()
    for k in range(depth):
        for a in range(count):
            x_step[a, k].wait_recv()
            slot = place(lax.rem(z + depth - k, depth), 1 - x, core)
            core_step[a, depth + k] = copy(
                a, outs[a].at[slot], slot, 3 * depth - 1 + k, sibling
            )
            core_step[a, depth + k].start()
    for a in range(count):
        for k in range(2 * depth):
            core_step[a, k].wait_recv()
        own[a].wait()
        for step in (z_step, x_step, core_step):
            for key, made in step.items():
                if key[0] == a:
                    made.wait_send()


def gather_rows(number, *blocks):
    experts = lax.axis_size("expert")
    depth, count = experts // 4, len(blocks)
    moved = sum(experts * b.size * b.dtype.itemsize for b in blocks)
    return pl.pallas_call(
        functools.partial(gather_kernel, depth, count),
        out_shape=[jax.ShapeDtypeStruct((experts, *b.shape), b.dtype) for b in blocks],
        in_specs=[pl.BlockSpec(memory_space=pl.ANY)] * count,
        out_specs=[pl.BlockSpec(memory_space=pl.ANY)] * count,
        scratch_shapes=[
            pltpu.SemaphoreType.DMA((count, 4 * depth - 1)),
            pltpu.SemaphoreType.DMA((count, 4 * depth - 1)),
            pltpu.SemaphoreType.DMA((count,)),
        ],
        compiler_params=pltpu.CompilerParams(collective_id=number, has_side_effects=True),
        cost_estimate=pl.CostEstimate(flops=0, bytes_accessed=16 * moved, transcendentals=0),
    )(*blocks)


def scatter_sum(rows):
    parts = lax.all_to_all(
        rows.reshape(lax.axis_size("expert"), -1, rows.shape[1]), "expert", 0, 0, tiled=True
    )
    return jnp.sum(parts.astype(jnp.float32), axis=0).astype(jnp.bfloat16)


def swap_pieces(block):
    return lax.ppermute(block, "dp", [(0, 1), (1, 0)])


def shards_dense(tokens, expert_ids, route_weights, cotangent, w_gate, w_up, w_down):
    tok_rows, feat_width = tokens.shape
    expert_count = lax.axis_size("expert")
    chunks = CHUNKS
    step = tok_rows // chunks
    me = lax.axis_index("expert")
    named = expert_ids[:, :, None] == jnp.arange(expert_count, dtype=jnp.int32)[None, None, :]
    dense = jnp.sum(jnp.where(named, route_weights[:, :, None], 0.0), axis=1)
    lanes = jnp.pad(dense, ((0, 0), (0, 128 - expert_count)))
    all_x, all_weights = gather_rows(0, tokens, lanes)
    mine = lax.dynamic_slice_in_dim(all_weights, me, 1, axis=2)
    gate_local, up_local, down_local = w_gate[0], w_up[0], w_down[0]
    last = (((1,), (1,)), ((), ()))
    first = (((0,), (0,)), ((), ()))
    f32 = jnp.float32

    def part(whole, c):
        return whole[:, c * step : (c + 1) * step].reshape(expert_count * step, -1)

    xs = [part(all_x, c) for c in range(chunks)]
    ws = [part(mine, c) for c in range(chunks)]
    gate_parts = [
        jnp.dot(x, gate_local, preferred_element_type=f32).astype(jnp.bfloat16) for x in xs
    ]
    cotangent, *gate_parts = lax.optimization_barrier((cotangent, *gate_parts))
    (all_dy,) = gather_rows(1, cotangent)
    cs = [part(all_dy, c) for c in range(chunks)]
    hiddens, dys, mixed, token_grad = [], [], [], []
    for c in range(chunks):
        rows_x = xs[c]
        gate_part = gate_parts[c]
        gate_other = swap_pieces(gate_part)
        up_part = jnp.dot(rows_x, up_local, preferred_element_type=f32).astype(jnp.bfloat16)
        up_other = swap_pieces(up_part)
        rows_dy = (cs[c].astype(f32) * ws[c]).astype(jnp.bfloat16)
        back_part = lax.dot_general(rows_dy, down_local, last, preferred_element_type=f32).astype(
            jnp.bfloat16
        )
        back_other = swap_pieces(back_part)
        hidden, grad_gate, grad_up = pointwise(
            gate_part.astype(f32) + gate_other.astype(f32),
            up_part.astype(f32) + up_other.astype(f32),
            back_part.astype(f32) + back_other.astype(f32),
        )
        out = jnp.dot(hidden, down_local, preferred_element_type=f32)
        mixed.append(scatter_sum((out * ws[c]).astype(jnp.bfloat16)))
        grad = lax.dot_general(grad_gate, gate_local, last, preferred_element_type=f32)
        grad = grad + lax.dot_general(grad_up, up_local, last, preferred_element_type=f32)
        token_grad.append(scatter_sum(grad.astype(jnp.bfloat16)))
        hiddens.append(hidden)
        dys.append(rows_dy)
    down_grad = lax.dot_general(
        jnp.concatenate(hiddens, axis=0),
        jnp.concatenate(dys, axis=0),
        first,
        preferred_element_type=f32,
    ).astype(jnp.bfloat16)
    return (
        jnp.concatenate(mixed, axis=0),
        jnp.concatenate(token_grad, axis=0),
        down_grad[None],
    )


def shards(tokens, expert_ids, *rest):
    tok_rows, top_count = expert_ids.shape
    expert_count = lax.axis_size("expert")
    capacity = min(tok_rows, 2 * tok_rows * top_count // expert_count)
    body = shards_dense if capacity == tok_rows else shards_slots
    return body(tokens, expert_ids, *rest)


def solution(mesh):
    return jax.shard_map(
        shards,
        mesh=mesh,
        in_specs=(
            P("expert", "dp"),
            P("expert", None),
            P("expert", None),
            P("expert", "dp"),
            P("expert", "dp", None),
            P("expert", "dp", None),
            P("expert", None, "dp"),
        ),
        out_specs=(P("expert", "dp"), P("expert", "dp"), P("expert", None, "dp")),
        check_vma=False,
    )
```

```python
import functools

import jax
import jax.numpy as jnp
from jax import lax
from jax.experimental import pallas as pl
from jax.experimental.pallas import tpu as pltpu
from jax.sharding import PartitionSpec as P


def pointwise(gate_pre, up_pre, grad_hidden):
    sigmoid_g = jax.nn.sigmoid(gate_pre)
    activation = gate_pre * sigmoid_g
    hidden = (activation * up_pre).astype(jnp.bfloat16)
    slope = sigmoid_g * (1.0 + gate_pre * (1.0 - sigmoid_g))
    grad_gate = (grad_hidden * up_pre * slope).astype(jnp.bfloat16)
    grad_up = (grad_hidden * activation).astype(jnp.bfloat16)
    return (hidden, grad_gate, grad_up)


def split_sums(full_sums, hidden_width):
    return pointwise(
        full_sums[:, :hidden_width],
        full_sums[:, hidden_width : 2 * hidden_width],
        full_sums[:, 2 * hidden_width :],
    )


def shards_slots(tokens, expert_ids, route_weights, cotangent, w_gate, w_up, w_down):
    tok_rows, feat_width = tokens.shape
    top_count = expert_ids.shape[1]
    expert_count = lax.axis_size("expert")
    capacity = min(tok_rows, 2 * tok_rows * top_count // expert_count)
    slots_total = expert_count * capacity
    pair_count = tok_rows * top_count
    flat_ids = expert_ids.reshape(pair_count)
    onehot = (flat_ids[:, None] == jnp.arange(expert_count, dtype=jnp.int32)[None, :]).astype(
        jnp.int32
    )
    position = jnp.sum((jnp.cumsum(onehot, axis=0) - onehot) * onehot, axis=1)
    slot_index = flat_ids * capacity + position
    chosen = slot_index[:, None] == jnp.arange(slots_total, dtype=jnp.int32)[None, :]
    chosen_b = chosen.astype(jnp.bfloat16)
    x_pairs = jnp.repeat(tokens, top_count, axis=0)
    pair_weights = route_weights.reshape(pair_count, 1)
    dy_pairs = (jnp.repeat(cotangent, top_count, axis=0).astype(jnp.float32) * pair_weights).astype(
        jnp.bfloat16
    )
    contract_pairs = (((0,), (0,)), ((), ()))
    send_x = lax.dot_general(
        chosen_b, x_pairs, contract_pairs, preferred_element_type=jnp.float32
    ).astype(jnp.bfloat16)
    send_dy = lax.dot_general(
        chosen_b, dy_pairs, contract_pairs, preferred_element_type=jnp.float32
    ).astype(jnp.bfloat16)
    recv_x, recv_dy = (
        lax.all_to_all(
            send_x.reshape(expert_count, capacity, feat_width),
            "expert",
            split_axis=0,
            concat_axis=0,
            tiled=True,
        ),
        lax.all_to_all(
            send_dy.reshape(expert_count, capacity, feat_width),
            "expert",
            split_axis=0,
            concat_axis=0,
            tiled=True,
        ),
    )
    rows_x = recv_x.reshape(slots_total, feat_width)
    rows_dy = recv_dy.reshape(slots_total, feat_width)
    gate_local = w_gate[0]
    up_local = w_up[0]
    down_local = w_down[0]
    hidden_width = gate_local.shape[1]
    contract_last = (((1,), (1,)), ((), ()))
    gate_part = jnp.dot(rows_x, gate_local, preferred_element_type=jnp.float32)
    up_part = jnp.dot(rows_x, up_local, preferred_element_type=jnp.float32)
    back_part = lax.dot_general(
        rows_dy, down_local, contract_last, preferred_element_type=jnp.float32
    )
    row_share = lax.psum_scatter(
        jnp.concatenate([gate_part, up_part, back_part], axis=1).astype(jnp.bfloat16),
        "dp",
        scatter_dimension=0,
        tiled=True,
    ).astype(jnp.float32)
    hidden_s, gate_s, up_s = split_sums(row_share, hidden_width)
    hidden, grad_gate, grad_up = (
        lax.all_gather(hidden_s, "dp", axis=0, tiled=True),
        lax.all_gather(gate_s, "dp", axis=0, tiled=True),
        lax.all_gather(up_s, "dp", axis=0, tiled=True),
    )
    expert_out = jnp.dot(hidden, down_local, preferred_element_type=jnp.float32).astype(
        jnp.bfloat16
    )
    grad_rows = lax.dot_general(
        grad_gate, gate_local, contract_last, preferred_element_type=jnp.float32
    )
    grad_rows = (
        grad_rows
        + lax.dot_general(grad_up, up_local, contract_last, preferred_element_type=jnp.float32)
    ).astype(jnp.bfloat16)
    down_grad = lax.dot_general(
        hidden, rows_dy, contract_pairs, preferred_element_type=jnp.float32
    ).astype(jnp.bfloat16)
    back_out, back_grad = (
        lax.all_to_all(
            expert_out.reshape(expert_count, capacity, feat_width),
            "expert",
            split_axis=0,
            concat_axis=0,
            tiled=True,
        ),
        lax.all_to_all(
            grad_rows.reshape(expert_count, capacity, feat_width),
            "expert",
            split_axis=0,
            concat_axis=0,
            tiled=True,
        ),
    )
    weighted_sel = (
        (chosen.astype(jnp.float32) * pair_weights)
        .reshape(tok_rows, top_count, slots_total)
        .sum(axis=1)
    )
    plain_sel = chosen_b.reshape(tok_rows, top_count, slots_total).sum(axis=1)
    mixed = jnp.dot(
        weighted_sel,
        back_out.reshape(slots_total, feat_width).astype(jnp.float32),
        precision=lax.Precision.HIGHEST,
    ).astype(jnp.bfloat16)
    token_grad = jnp.dot(
        plain_sel, back_grad.reshape(slots_total, feat_width), preferred_element_type=jnp.float32
    ).astype(jnp.bfloat16)
    return (mixed, token_grad, down_grad[None])


CHUNKS = 2


def gather_kernel(depth, count, *refs):
    ins, outs = refs[:count], refs[count : 2 * count]
    send_sem, recv_sem, own_sem = refs[2 * count :]
    me, piece = lax.axis_index("expert"), lax.axis_index("dp")
    z, x, core = me // 4, (me // 2) % 2, me % 2

    def place(z_at, x_at, core_at):
        return (z_at * 2 + x_at) * 2 + core_at

    across, sibling = place(z, 1 - x, core), place(z, x, 1 - core)
    along = [place(lax.rem(z + k, depth), x, core) for k in range(1, depth)]
    barrier = pltpu.get_barrier_semaphore()
    for peer in [*along, across, sibling]:
        pl.semaphore_signal(
            barrier, inc=1, device_id=(piece, peer), device_id_type=pl.DeviceIdType.MESH
        )
    pl.semaphore_wait(barrier, depth + 1)

    def copy(a, src, slot, sem, peer):
        return pltpu.make_async_remote_copy(
            src_ref=src,
            dst_ref=outs[a].at[slot],
            send_sem=send_sem.at[a, sem],
            recv_sem=recv_sem.at[a, sem],
            device_id=(piece, peer),
            device_id_type=pl.DeviceIdType.MESH,
        )

    own, started = [], []
    x_step = {}
    core_step = {}
    z_step = {}
    for a in range(count):
        own.append(pltpu.make_async_copy(ins[a], outs[a].at[me], own_sem.at[a]))
        own[-1].start()
        for k in range(1, depth):
            z_step[a, k] = copy(a, ins[a], me, k - 1, along[k - 1])
            z_step[a, k].start()
        x_step[a, 0] = copy(a, ins[a], me, depth - 1, across)
        x_step[a, 0].start()
        core_step[a, 0] = copy(a, ins[a], me, 2 * depth - 1, sibling)
        core_step[a, 0].start()
    for k in range(1, depth):
        for a in range(count):
            z_step[a, k].wait_recv()
            slot = place(lax.rem(z + depth - k, depth), x, core)
            x_step[a, k] = copy(a, outs[a].at[slot], slot, depth - 1 + k, across)
            x_step[a, k].start()
            core_step[a, k] = copy(a, outs[a].at[slot], slot, 2 * depth - 1 + k, sibling)
            core_step[a, k].start()
    for k in range(depth):
        for a in range(count):
            x_step[a, k].wait_recv()
            slot = place(lax.rem(z + depth - k, depth), 1 - x, core)
            core_step[a, depth + k] = copy(
                a, outs[a].at[slot], slot, 3 * depth - 1 + k, sibling
            )
            core_step[a, depth + k].start()
    for a in range(count):
        for k in range(2 * depth):
            core_step[a, k].wait_recv()
        own[a].wait()
        for step in (z_step, x_step, core_step):
            for key, made in step.items():
                if key[0] == a:
                    made.wait_send()


def gather_rows(number, *blocks):
    experts = lax.axis_size("expert")
    depth, count = experts // 4, len(blocks)
    moved = sum(experts * b.size * b.dtype.itemsize for b in blocks)
    return pl.pallas_call(
        functools.partial(gather_kernel, depth, count),
        out_shape=[jax.ShapeDtypeStruct((experts, *b.shape), b.dtype) for b in blocks],
        in_specs=[pl.BlockSpec(memory_space=pl.ANY)] * count,
        out_specs=[pl.BlockSpec(memory_space=pl.ANY)] * count,
        scratch_shapes=[
            pltpu.SemaphoreType.DMA((count, 4 * depth - 1)),
            pltpu.SemaphoreType.DMA((count, 4 * depth - 1)),
            pltpu.SemaphoreType.DMA((count,)),
        ],
        compiler_params=pltpu.CompilerParams(collective_id=number, has_side_effects=True),
        cost_estimate=pl.CostEstimate(flops=0, bytes_accessed=16 * moved, transcendentals=0),
    )(*blocks)


def scatter_kernel(depth, count, *refs):
    ins, outs, rest = refs[:count], refs[count : 2 * count], refs[2 * count :]
    from_core, core_sum, from_x, x_sum, from_z, send_sem, recv_sem = rest
    me, piece = lax.axis_index("expert"), lax.axis_index("dp")
    z, x, core = me // 4, (me // 2) % 2, me % 2
    f32 = jnp.float32

    def place(z_at, x_at, core_at):
        return (z_at * 2 + x_at) * 2 + core_at

    across, sibling = place(z, 1 - x, core), place(z, x, 1 - core)
    along = [place(lax.rem(z + k, depth), x, core) for k in range(1, depth)]
    barrier = pltpu.get_barrier_semaphore()
    for peer in [*along, across, sibling]:
        pl.semaphore_signal(
            barrier, inc=1, device_id=(piece, peer), device_id_type=pl.DeviceIdType.MESH
        )
    pl.semaphore_wait(barrier, depth + 1)

    def copy(a, src, dst, sem, peer):
        made = pltpu.make_async_remote_copy(
            src_ref=src,
            dst_ref=dst,
            send_sem=send_sem.at[a, sem],
            recv_sem=recv_sem.at[a, sem],
            device_id=(piece, peer),
            device_id_type=pl.DeviceIdType.MESH,
        )
        made.start()
        return made

    core_step = [
        copy(a, ins[a].at[:, :, 1 - core], from_core.at[a], 0, sibling) for a in range(count)
    ]
    x_step, z_step = [], []
    for a in range(count):
        core_step[a].wait_recv()

        @pl.loop(0, depth)
        def _(k):
            core_sum[a, k] = (
                ins[a][k, :, core].astype(f32) + from_core[a, k].astype(f32)
            ).astype(jnp.bfloat16)

        x_step.append(copy(a, core_sum.at[a, :, 1 - x], from_x.at[a], 1, across))
    for a in range(count):
        x_step[a].wait_recv()

        @pl.loop(0, depth)
        def _(k):
            x_sum[a, k] = (
                core_sum[a, k, x].astype(f32) + from_x[a, k].astype(f32)
            ).astype(jnp.bfloat16)

        for k in range(1, depth):
            target = x_sum.at[a, lax.rem(z + k, depth)]
            z_step.append(copy(a, target, from_z.at[a, k - 1], 1 + k, along[k - 1]))
    for a in range(count):
        total = x_sum[a, z].astype(f32)
        for k in range(depth - 1):
            z_step[a * (depth - 1) + k].wait_recv()
            total = total + from_z[a, k].astype(f32)
        outs[a][...] = total.astype(jnp.bfloat16)
    for made in [*core_step, *x_step, *z_step]:
        made.wait_send()


def scatter_sum(number, *blocks):
    experts = lax.axis_size("expert")
    depth, count = experts // 4, len(blocks)
    rows, width = blocks[0].shape[0] // experts, blocks[0].shape[1]
    b16 = jnp.bfloat16
    return pl.pallas_call(
        functools.partial(scatter_kernel, depth, count),
        out_shape=[jax.ShapeDtypeStruct((rows, width), b16)] * count,
        in_specs=[pl.BlockSpec(memory_space=pltpu.VMEM)] * count,
        out_specs=[pl.BlockSpec(memory_space=pltpu.VMEM)] * count,
        scratch_shapes=[
            pltpu.VMEM((count, depth, 2, rows, width), b16),
            pltpu.VMEM((count, depth, 2, rows, width), b16),
            pltpu.VMEM((count, depth, rows, width), b16),
            pltpu.VMEM((count, depth, rows, width), b16),
            pltpu.VMEM((count, depth - 1, rows, width), b16),
            pltpu.SemaphoreType.DMA((count, depth + 1)),
            pltpu.SemaphoreType.DMA((count, depth + 1)),
        ],
        compiler_params=pltpu.CompilerParams(
            collective_id=number, has_side_effects=True, vmem_limit_bytes=24 << 20
        ),
    )(*[b.reshape(depth, 2, 2, rows, width) for b in blocks])


def swap_pieces(block):
    return lax.ppermute(block, "dp", [(0, 1), (1, 0)])


def shards_dense(tokens, expert_ids, route_weights, cotangent, w_gate, w_up, w_down):
    tok_rows, feat_width = tokens.shape
    expert_count = lax.axis_size("expert")
    chunks = CHUNKS
    step = tok_rows // chunks
    me = lax.axis_index("expert")
    named = expert_ids[:, :, None] == jnp.arange(expert_count, dtype=jnp.int32)[None, None, :]
    dense = jnp.sum(jnp.where(named, route_weights[:, :, None], 0.0), axis=1)
    lanes = jnp.pad(dense, ((0, 0), (0, 128 - expert_count)))
    all_x, all_weights = gather_rows(0, tokens, lanes)
    mine = lax.dynamic_slice_in_dim(all_weights, me, 1, axis=2)
    gate_local, up_local, down_local = w_gate[0], w_up[0], w_down[0]
    last = (((1,), (1,)), ((), ()))
    first = (((0,), (0,)), ((), ()))
    f32 = jnp.float32

    def part(whole, c):
        return whole[:, c * step : (c + 1) * step].reshape(expert_count * step, -1)

    xs = [part(all_x, c) for c in range(chunks)]
    ws = [part(mine, c) for c in range(chunks)]
    gate_parts = [
        jnp.dot(x, gate_local, preferred_element_type=f32).astype(jnp.bfloat16) for x in xs
    ]
    cotangent, *gate_parts = lax.optimization_barrier((cotangent, *gate_parts))
    (all_dy,) = gather_rows(1, cotangent)
    cs = [part(all_dy, c) for c in range(chunks)]
    gate_others = [swap_pieces(p) for p in gate_parts]
    up_parts = [
        jnp.dot(x, up_local, preferred_element_type=f32).astype(jnp.bfloat16) for x in xs
    ]
    up_others = [swap_pieces(p) for p in up_parts]
    dys = [(r.astype(f32) * w).astype(jnp.bfloat16) for r, w in zip(cs, ws)]
    back_parts = [
        lax.dot_general(r, down_local, last, preferred_element_type=f32).astype(jnp.bfloat16)
        for r in dys
    ]
    back_others = [swap_pieces(p) for p in back_parts]
    held = back_parts
    for c in range(chunks):
        gate_others[c], up_others[c], held = lax.optimization_barrier(
            (gate_others[c], up_others[c], held)
        )
    hiddens, outs, grads = [], [], []
    for c in range(chunks):
        hidden, grad_gate, grad_up = pointwise(
            gate_parts[c].astype(f32) + gate_others[c].astype(f32),
            up_parts[c].astype(f32) + up_others[c].astype(f32),
            held[c].astype(f32) + back_others[c].astype(f32),
        )
        out = jnp.dot(hidden, down_local, preferred_element_type=f32)
        grad = lax.dot_general(grad_gate, gate_local, last, preferred_element_type=f32)
        grad = grad + lax.dot_general(grad_up, up_local, last, preferred_element_type=f32)
        outs.append((out * ws[c]).astype(jnp.bfloat16))
        grads.append(grad.astype(jnp.bfloat16))
        hiddens.append(hidden)
    mixed = scatter_sum(2, *outs)
    token_grad = scatter_sum(3, *grads)
    down_grad = lax.dot_general(
        jnp.concatenate(hiddens, axis=0),
        jnp.concatenate(dys, axis=0),
        first,
        preferred_element_type=f32,
    ).astype(jnp.bfloat16)
    return (
        jnp.concatenate(mixed, axis=0),
        jnp.concatenate(token_grad, axis=0),
        down_grad[None],
    )


def shards(tokens, expert_ids, *rest):
    tok_rows, top_count = expert_ids.shape
    expert_count = lax.axis_size("expert")
    capacity = min(tok_rows, 2 * tok_rows * top_count // expert_count)
    body = shards_dense if capacity == tok_rows else shards_slots
    return body(tokens, expert_ids, *rest)


def solution(mesh):
    return jax.shard_map(
        shards,
        mesh=mesh,
        in_specs=(
            P("expert", "dp"),
            P("expert", None),
            P("expert", None),
            P("expert", "dp"),
            P("expert", "dp", None),
            P("expert", "dp", None),
            P("expert", None, "dp"),
        ),
        out_specs=(P("expert", "dp"), P("expert", "dp"), P("expert", None, "dp")),
        check_vma=False,
    )
```
